1024 devices in a mesh: grid: 32 (over x, z_lo), interp: 32 (over y, z_hi, core).
Axes of the slice: x: 8, y: 8, z: 8 (z_hi: 2, z_lo: 4; z = z_hi * 4 + z_lo), core: 2. Of those that a mesh axis runs over, the one named last changes fastest.
Arguments:
- valence: bfloat16 [262144, 512], P(('grid', 'interp')), may hold values from -1.296875 to 1.296875
- conduction: bfloat16 [262144, 512], P(('grid', 'interp')), may hold values from -1.296875 to 1.296875
- points: int32 [16384], P('grid'), may hold values from 0 to 262143, as said below
- inverse_metric: bfloat16 [16384, 16384], P('grid', 'interp'), as said below
Outputs:
- fitting: bfloat16 [1024, 16384], P('grid', 'interp')
The draws below stay inside these ranges and needn't reach their ends.
Inputs may be any that keep to these rules, and one draw needn't show every extreme that they name: Entries k * 512 to (k + 1) * 512 - 1 of points are distinct grid points of slab k, that is of k * 8192 to (k + 1) * 8192 - 1, and include that slab's first and last point. `inverse_metric`: A diagonal between 0.5 and 2 with small dense entries off it, of standard deviation about 0.5 / sqrt(16384).
All inputs are finite; a program needn't handle non-finite values.
Results may differ from the reference program's by a relative error of at most 0.0048.
Values may be sent and summed in bfloat16 or wider, within the bound.
A program may use at most 32 MiB of HBM per device.

```python
import jax
import jax.numpy as jnp
from jax import lax

NV = 512
NC = 512
NMU = 16384
BLK_DEV = 1
GRID_PTS = 256
NGRID = 262144
SLAB = 8192
ROWS = 1024
MU_BLK = 512


def draw_points(key, part):
    block_count = NMU // MU_BLK

    def one_block(block_key, slab_index):
        first_key, second_key = jax.random.split(block_key)
        inner = jax.random.permutation(first_key, SLAB - 2)[:MU_BLK - 2] + 1
        whole = jnp.concatenate([jnp.zeros((1,), jnp.int32), jnp.full((1,), SLAB - 1, jnp.int32), inner.astype(jnp.int32)])
        whole = jax.random.permutation(second_key, whole)
        return whole + slab_index * SLAB
    block_keys = jax.random.split(jax.random.fold_in(key, 11), block_count)
    slabs = jnp.arange(block_count, dtype=jnp.int32)
    return jax.vmap(one_block)(block_keys, slabs).reshape(NMU).astype(jnp.int32)


def draw_inverse_metric(key, part):
    diag_key, off_key = jax.random.split(jax.random.fold_in(key, 23))
    row_ids = jnp.arange(NMU, dtype=jnp.int32)[:, None]
    col_ids = jnp.arange(NMU, dtype=jnp.int32)[None, :]
    diag_vals = jnp.exp(jax.random.uniform(diag_key, (NMU, 1), jnp.float32, -0.69, 0.69))
    off_vals = jax.random.normal(off_key, (NMU, NMU), jnp.float32) * (0.5 / NMU ** 0.5)
    whole = jnp.where(row_ids == col_ids, diag_vals, off_vals)
    return whole.astype(jnp.bfloat16)


def shard_levels(key, extent, cuts, least, high):
    loudness = 1.0
    for axis_at, shards_of in cuts:
        steps = jax.random.uniform(jax.random.fold_in(jax.random.fold_in(key, 6), axis_at), (shards_of,), jnp.float32, least / len(cuts), high / len(cuts))
        loudness = loudness * jnp.repeat(jnp.exp(steps), extent[axis_at] // shards_of).reshape((-1,) + (1,) * (len(extent) - 1 - axis_at))
    return loudness


def bell_draw(own_key, shape, scale, most, pieces=(), kind=jnp.bfloat16):
    array = scale * jax.random.normal(own_key, shape, jnp.float32)
    if pieces:
        array = array * shard_levels(own_key, shape, pieces, -0.22, 0.18)
    return jnp.clip(array, -most, most).astype(kind)


def setup_inputs(seed: int = 0) -> dict:
    key_list = jax.random.split(jax.random.key(seed), 5)
    valence = bell_draw(key_list[0], (NGRID, NV), 0.21, 1.296875, ((0, 1024),))
    conduction = bell_draw(key_list[1], (NGRID, NC), 0.21, 1.296875, ((0, 1024),))
    points = draw_points(jax.random.fold_in(key_list[4], 71), 0)
    inverse_metric = draw_inverse_metric(jax.random.fold_in(key_list[4], 71), 0)
    return {"valence": valence, "conduction": conduction, "points": points, "inverse_metric": inverse_metric}


def reference(valence, conduction, points, inverse_metric):
    devices_total = NGRID // GRID_PTS
    block_val = valence.reshape(devices_total, GRID_PTS, NV)[:, :BLK_DEV].reshape(ROWS, NV)
    block_con = conduction.reshape(devices_total, GRID_PTS, NC)[:, :BLK_DEV].reshape(ROWS, NC)
    point_val = jnp.take(valence, points, axis=0)
    point_con = jnp.take(conduction, points, axis=0)
    dims = (((1,), (1,)), ((), ()))
    gram_val = lax.dot_general(block_val, point_val, dims, preferred_element_type=jnp.float32)
    gram_con = lax.dot_general(block_con, point_con, dims, preferred_element_type=jnp.float32)
    pair = (gram_val * gram_con).astype(jnp.bfloat16)
    return jnp.dot(pair, inverse_metric, preferred_element_type=jnp.float32).astype(jnp.bfloat16)
```

```python
import jax
import jax.numpy as jnp
from jax import lax
from jax.experimental import pallas as pl
from jax.experimental.pallas import tpu as pltpu
from jax.sharding import PartitionSpec as P

MESH = pl.DeviceIdType.MESH
BF16, F32 = jnp.bfloat16, jnp.float32

NX, NZL, NY = 8, 4, 8
COPIES = 3 + 3 * (NY - 1) + (NZL - 1) + 3 * (NX - 1) + 3 + (NY - 1) + (2 * NZL - 1)


def kernel(
    pts_ref, val_ref, con_ref, met_ref, out_ref,
    val_mate, con_mate, met_mate, row_buf, zl_buf, blk_buf,
    pick_buf, pick_in, pick_z, pts_buf, pair_buf, part_buf, part_in, sum_buf, sum_in,
    send_sem, recv_sem,
):
    g, i = lax.axis_index("grid"), lax.axis_index("interp")
    x, zl = lax.div(g, NZL), lax.rem(g, NZL)
    y, zh, c = lax.div(i, 4), lax.rem(lax.div(i, 2), 2), lax.rem(i, 2)
    rows, width = val_ref.shape
    half = pts_ref.shape[1] // 2
    piece = half // NY
    mate = 1 - c

    def device(x=x, zl=zl, y=y, zh=zh, c=c):
        return (x * NZL + zl, y * 4 + zh * 2 + c)

    y_peers = [device(y=lax.rem(y + k, NY)) for k in range(1, NY)]
    x_peers = [device(x=lax.rem(x + k, NX)) for k in range(1, NX)]
    zl_peers = [device(zl=lax.rem(zl + k, NZL)) for k in range(1, NZL)]
    zl_mates = [device(zl=lax.rem(zl + k, NZL), c=mate) for k in range(1, NZL)]
    z_peer, core_peer = device(zh=1 - zh), device(c=mate)

    barrier = pltpu.get_barrier_semaphore()
    peers = [core_peer, z_peer] + y_peers + x_peers + zl_peers + zl_mates
    for peer in peers:
        pl.semaphore_signal(barrier, inc=1, device_id=peer, device_id_type=MESH)

    copies = []

    def send(src, dst, peer):
        n = len(copies)
        copy = pltpu.make_async_remote_copy(
            src_ref=src,
            dst_ref=dst,
            send_sem=send_sem.at[n],
            recv_sem=recv_sem.at[n],
            device_id=peer,
            device_id_type=MESH,
        )
        copy.start()
        copies.append(copy)
        return copy

    row_buf[y] = jnp.concatenate([val_ref[0:1, :], con_ref[0:1, :]], axis=1).astype(F32)

    pts = pts_ref[:, pl.ds(pl.multiple_of(c * half, half), half)]
    spread = jnp.broadcast_to(pts, (128, half)).T

    def picked(owner, val, con):
        local = spread - owner * rows
        lane = lax.broadcasted_iota(jnp.int32, (half, 128), 1)
        hot = jnp.concatenate(
            [jnp.where(local == lane + at, 1.0, 0.0) for at in range(0, rows, 128)], axis=1
        ).astype(BF16)
        return [
            jnp.dot(hot, ref[...], preferred_element_type=F32).astype(BF16).reshape(NY, piece, width)
            for ref in (val, con)
        ]

    own = g * (NY * 4) + i
    pick_val, pick_con = picked(own, val_ref, con_ref)
    pick_buf[:, :, :width] = pick_val
    pick_buf[:, :, width:] = pick_con

    pl.semaphore_wait(barrier, len(peers))

    core_rows = [send(val_ref, val_mate, core_peer), send(con_ref, con_mate, core_peer)]
    row_copies = [send(row_buf.at[y], row_buf.at[y], peer) for peer in y_peers]
    core_met = send(met_ref, met_mate, core_peer)

    for copy in core_rows:
        copy.wait_recv()
    pick_val, pick_con = picked(own - c + mate, val_mate, con_mate)
    pick_buf[:, :, :width] += pick_val
    pick_buf[:, :, width:] += pick_con
    pick_copies = [
        send(pick_buf.at[lax.rem(y + k, NY)], pick_in.at[k - 1], y_peers[k - 1])
        for k in range(1, NY)
    ]

    for copy in row_copies:
        copy.wait_recv()
    for k in range(NY):
        zl_buf[zl, k : k + 1, :] = row_buf[k]
    zl_copies = [send(zl_buf.at[zl], zl_buf.at[zl], peer) for peer in zl_peers]
    for copy in zl_copies:
        copy.wait_recv()
    blk_buf[x] = zl_buf[...].reshape(NZL * NY, 2 * width).astype(BF16)
    blk_copies = [send(blk_buf.at[x], blk_buf.at[x], peer) for peer in x_peers]

    for copy in pick_copies:
        copy.wait_recv()
    total = pick_buf[y].astype(F32)
    for k in range(NY - 1):
        total += pick_in[k].astype(F32)
    pts_buf[c] = total.astype(BF16)
    z_copy = send(pts_buf.at[c], pick_z, z_peer)
    z_copy.wait_recv()
    z_copy.wait_send()
    pts_buf[c] = (total + pick_z[...].astype(F32)).astype(BF16)
    core_copy = send(pts_buf.at[c], pts_buf.at[c], core_peer)
    core_copy.wait_recv()
    for copy in blk_copies:
        copy.wait_recv()

    block = blk_buf[...].reshape(NX * NZL * NY, 2 * width)
    points = pts_buf[...].reshape(2 * piece, 2 * width)
    across = (((1,), (1,)), ((), ()))
    gram_val = lax.dot_general(points[:, :width], block[:, :width], across, preferred_element_type=F32)
    gram_con = lax.dot_general(points[:, width:], block[:, width:], across, preferred_element_type=F32)
    pair = (gram_val * gram_con).astype(BF16)
    pair_buf[zh, :, y] = pair.reshape(2, piece, NX * NZL * NY)

    mine, theirs = pair_buf.at[zh, :, y], pair_buf.at[1 - zh, :, y]
    pair_z = send(mine, mine, z_peer)
    pair_copies = [send(mine, mine, peer) for peer in y_peers]
    pair_z.wait_recv()
    pair_copies += [send(theirs, theirs, peer) for peer in y_peers]
    core_met.wait_recv()
    for copy in pair_copies:
        copy.wait_recv()

    down = (((0,), (0,)), ((), ()))
    part_copies = []
    for metric, to_core in ((met_mate, mate), (met_ref, c)):
        for q in range(2):
            pair_q = pair_buf[q].reshape(2 * half, NX * NZL * NY)
            part = lax.dot_general(pair_q, metric[...], down, preferred_element_type=F32)
            part_buf[to_core, :, q] = part.astype(BF16).reshape(NX, NZL * NY, width)
        part_copies += [
            send(
                part_buf.at[to_core, lax.rem(x + k, NX)],
                part_in.at[k - 1, to_core],
                x_peers[k - 1],
            )
            for k in range(1, NX)
        ]
    for copy in part_copies:
        copy.wait_recv()

    for to_core in range(2):
        sums = []
        for q in range(2):
            s = part_buf[to_core, x, q].astype(F32)
            for k in range(NX - 1):
                s += part_in[k, to_core, q].astype(F32)
            sums.append(s)
        for to_zl in range(NZL):
            at = to_zl * NY
            sum_buf[to_zl, to_core] = jnp.concatenate(
                [s[at : at + NY] for s in sums], axis=0
            ).astype(BF16)
    sum_copies = []
    for k in range(NZL):
        for dc in range(2):
            if k or dc:
                to_zl = lax.rem(zl + k, NZL)
                to_core = mate if dc else c
                sum_copies.append(
                    send(sum_buf.at[to_zl, to_core], sum_in.at[k, c], device(zl=to_zl, c=to_core))
                )
    sum_in[0, c] = sum_buf[zl, c]
    for copy in sum_copies:
        copy.wait_recv()
    for from_core in range(2):
        s = sum_in[0, from_core].astype(F32)
        for k in range(1, NZL):
            s += sum_in[k, from_core].astype(F32)
        out_ref[from_core] = s.reshape(2, NY, width)

    for n, copy in enumerate(copies):
        if copy is not z_copy:
            copy.wait_send()


def shards(valence, conduction, points, inverse_metric):
    rows, width = valence.shape
    count = points.shape[0]
    piece = count // 2 // NY
    lines = NX * NZL * NY
    vmem = pl.BlockSpec(memory_space=pltpu.VMEM)
    out = pl.pallas_call(
        kernel,
        out_shape=jax.ShapeDtypeStruct((2, 2, NY, width), F32),
        in_specs=[vmem] * 4,
        out_specs=vmem,
        scratch_shapes=[
            pltpu.VMEM((rows, width), BF16),
            pltpu.VMEM((rows, width), BF16),
            pltpu.VMEM((count, width), BF16),
            pltpu.VMEM((NY, 1, 2 * width), F32),
            pltpu.VMEM((NZL, NY, 2 * width), F32),
            pltpu.VMEM((NX, NZL * NY, 2 * width), BF16),
            pltpu.VMEM((NY, piece, 2 * width), BF16),
            pltpu.VMEM((NY - 1, piece, 2 * width), BF16),
            pltpu.VMEM((piece, 2 * width), BF16),
            pltpu.VMEM((2, piece, 2 * width), BF16),
            pltpu.VMEM((2, 2, NY, piece, lines), BF16),
            pltpu.VMEM((2, NX, 2, NZL * NY, width), BF16),
            pltpu.VMEM((NX - 1, 2, 2, NZL * NY, width), BF16),
            pltpu.VMEM((NZL, 2, 2 * NY, width), BF16),
            pltpu.VMEM((NZL, 2, 2 * NY, width), BF16),
            pltpu.SemaphoreType.DMA((COPIES,)),
            pltpu.SemaphoreType.DMA((COPIES,)),
        ],
        compiler_params=pltpu.CompilerParams(
            collective_id=0, has_side_effects=True, vmem_limit_bytes=40 * 2**20
        ),
    )(points[None, :], valence, conduction, inverse_metric)
    return out.transpose(2, 1, 0, 3).reshape(NY * 4, width).astype(BF16)


def solution(mesh):
    return jax.shard_map(
        shards,
        mesh=mesh,
        in_specs=(
            P(("grid", "interp"), None),
            P(("grid", "interp"), None),
            P("grid"),
            P("grid", "interp"),
        ),
        out_specs=P("grid", "interp"),
        check_vma=False,
    )
```

```python
import jax
import jax.numpy as jnp
from jax import lax
from jax.experimental import pallas as pl
from jax.experimental.pallas import tpu as pltpu
from jax.sharding import PartitionSpec as P

MESH = pl.DeviceIdType.MESH
BF16, F32 = jnp.bfloat16, jnp.float32

NX, NZL, NY = 8, 4, 8
COPIES = 112


def kernel(
    pts_hbm, val_hbm, con_hbm, met_hbm, out_ref,
    pts_ref, val_ref, con_ref, met_ref, val_mate, con_mate, met_mate, row_buf, zl_buf, blk_buf,
    pick_buf, pick_in, pick_z, pts_buf, pair_buf,
    px_buf, px_in, pz_buf, pz_in, sx_buf, sx_in, sz_buf, sz_in,
    send_sem, recv_sem, load_sem,
):
    g, i = lax.axis_index("grid"), lax.axis_index("interp")
    x, zl = lax.div(g, NZL), lax.rem(g, NZL)
    y, zh, c = lax.div(i, 4), lax.rem(lax.div(i, 2), 2), lax.rem(i, 2)
    rows, width = val_ref.shape
    half = pts_ref.shape[1] // 2
    piece = half // NY
    lines = NX * NZL * NY
    mate = 1 - c

    def device(x=x, zl=zl, y=y, zh=zh, c=c):
        return (x * NZL + zl, y * 4 + zh * 2 + c)

    y_peers = [device(y=lax.rem(y + k, NY)) for k in range(1, NY)]
    x_peers = [device(x=lax.rem(x + k, NX)) for k in range(1, NX)]
    zl_peers = [device(zl=lax.rem(zl + k, NZL)) for k in range(1, NZL)]
    zl_mates = [device(zl=lax.rem(zl + k, NZL), c=mate) for k in range(1, NZL)]
    z_peer, core_peer = device(zh=1 - zh), device(c=mate)

    barrier = pltpu.get_barrier_semaphore()
    peers = [core_peer, z_peer] + x_peers + y_peers + zl_peers + zl_mates
    for peer in peers:
        pl.semaphore_signal(barrier, inc=1, device_id=peer, device_id_type=MESH)

    loads = [
        pltpu.make_async_copy(src, dst, load_sem.at[n])
        for n, (src, dst) in enumerate(
            [(val_hbm, val_ref), (con_hbm, con_ref), (pts_hbm, pts_ref), (met_hbm, met_ref)]
        )
    ]
    for load in loads:
        load.start()

    copies = []

    def send(src, dst, peer):
        n = len(copies)
        copy = pltpu.make_async_remote_copy(
            src_ref=src,
            dst_ref=dst,
            send_sem=send_sem.at[n],
            recv_sem=recv_sem.at[n],
            device_id=peer,
            device_id_type=MESH,
        )
        copy.start()
        copies.append(copy)
        return copy

    for load in loads[:2]:
        load.wait()
    row_buf[y] = jnp.concatenate([val_ref[0:1, :], con_ref[0:1, :]], axis=1).astype(F32)

    pl.semaphore_wait(barrier, len(peers))

    row_copies = [send(row_buf.at[y], row_buf.at[y], peer) for peer in y_peers]
    core_rows = [send(val_ref, val_mate, core_peer), send(con_ref, con_mate, core_peer)]

    loads[2].wait()
    pts = pts_ref[:, pl.ds(pl.multiple_of(c * half, half), half)]
    spread = jnp.broadcast_to(pts, (128, half)).T

    def one_hot(owner):
        local = spread - owner * rows
        lane = lax.broadcasted_iota(jnp.int32, (half, 128), 1)
        return jnp.concatenate(
            [jnp.where(local == lane + at, 1.0, 0.0) for at in range(0, rows, 128)], axis=1
        ).astype(BF16)

    def picked(hot, ref):
        pick = jnp.dot(hot, ref[...], preferred_element_type=F32)
        return pick.astype(BF16).reshape(NY, piece, width)

    own = g * (NY * 4) + i
    hot, hot_mate = one_hot(own), one_hot(own - c + mate)

    for h, ref in enumerate((val_ref, con_ref)):
        pick_buf[h] = picked(hot, ref)
    pick_copies = []
    for h, ref in enumerate((val_mate, con_mate)):
        core_rows[h].wait_recv()
        pick_buf[h] += picked(hot_mate, ref)
        pick_copies.append([
            send(pick_buf.at[h, lax.rem(y + k, NY)], pick_in.at[h, k - 1], y_peers[k - 1])
            for k in range(1, NY)
        ])

    for copy in row_copies:
        copy.wait_recv()
    for k in range(NY):
        zl_buf[zl, k : k + 1, :] = row_buf[k]
    zl_copies = [send(zl_buf.at[zl], zl_buf.at[zl], peer) for peer in zl_peers]

    for copy in zl_copies:
        copy.wait_recv()
    blk_buf[x] = zl_buf[...].reshape(2, NZL * NY // 2, 2 * width).astype(BF16)
    blk_copies = [send(blk_buf.at[x], blk_buf.at[x], peer) for peer in x_peers]
    loads[3].wait()
    core_met = send(met_ref, met_mate, core_peer)

    z_copies = []
    for h in range(2):
        for copy in pick_copies[h]:
            copy.wait_recv()
        total = pick_buf[h, y].astype(F32)
        for k in range(NY - 1):
            total += pick_in[h, k].astype(F32)
        pts_buf[h, 0] = total.astype(BF16)
        z_copies.append(send(pts_buf.at[h, 0], pick_z.at[h], z_peer))
    core_copies = []
    for h in range(2):
        z_copies[h].wait_recv()
        pts_buf[h, 1 + c] = (pts_buf[h, 0].astype(F32) + pick_z[h].astype(F32)).astype(BF16)
        core_copies.append(send(pts_buf.at[h, 1 + c], pts_buf.at[h, 1 + c], core_peer))
    for copy in blk_copies:
        copy.wait_recv()

    across = (((1,), (1,)), ((), ()))
    block = blk_buf[...].reshape(lines, 2 * width)
    grams = []
    for h in range(2):
        core_copies[h].wait_recv()
        points = pts_buf[h, 1:].reshape(2 * piece, width)
        grams.append(
            lax.dot_general(
                points, block[:, h * width : (h + 1) * width], across, preferred_element_type=F32
            )
        )
    pair_buf[0, :, y] = (grams[0] * grams[1]).astype(BF16).reshape(2, piece, lines)

    mine, theirs = pair_buf.at[0, :, y], pair_buf.at[1, :, y]
    pair_z = send(mine, theirs, z_peer)
    pair_copies = [send(mine, mine, peer) for peer in y_peers]
    pair_z.wait_recv()
    pair_copies += [send(theirs, theirs, peer) for peer in y_peers]
    for copy in pair_copies:
        copy.wait_recv()
    core_met.wait_recv()

    down = (((0,), (0,)), ((), ()))

    def share(q, metric):
        pair_q = pair_buf[q].reshape(2 * half, lines)
        return lax.dot_general(pair_q, metric[...], down, preferred_element_type=F32)

    for q in range(2):
        part = share(q, met_mate)
        px_buf[:, q] = part.astype(BF16).reshape(NX, NZL * NY, width)
    px_copies = [
        send(px_buf.at[lax.rem(x + k, NX)], px_in.at[k - 1], x_peers[k - 1]) for k in range(1, NX)
    ]
    for q in range(2):
        part = share(q, met_ref).reshape(NX, NZL, NY, width)
        for k in range(NZL):
            pz_buf[k, q] = part[:, k].reshape(NX * NY, width).astype(BF16)
    pz_copies = [
        send(pz_buf.at[lax.rem(zl + k, NZL)], pz_in.at[k - 1], zl_peers[k - 1])
        for k in range(1, NZL)
    ]

    def summed(own, inbox, count):
        total = own.astype(F32)
        for k in range(count):
            total += inbox(k).astype(F32)
        return total

    for copy in pz_copies:
        copy.wait_recv()
    sums = [summed(pz_buf[zl, q], lambda k: pz_in[k, q], NZL - 1) for q in range(2)]
    for k in range(NX):
        sx_buf[k] = jnp.concatenate([s[k * NY : (k + 1) * NY] for s in sums], axis=0).astype(BF16)
    sx_copies = [
        send(sx_buf.at[lax.rem(x + k, NX)], sx_in.at[k - 1], x_peers[k - 1]) for k in range(1, NX)
    ]
    for copy in px_copies:
        copy.wait_recv()
    sums = [summed(px_buf[x, q], lambda k: px_in[k, q], NX - 1) for q in range(2)]
    for k in range(NZL):
        sz_buf[k] = jnp.concatenate([s[k * NY : (k + 1) * NY] for s in sums], axis=0).astype(BF16)
    sz_copies = [
        send(sz_buf.at[lax.rem(zl + k, NZL)], sz_in.at[k], device(zl=lax.rem(zl + k, NZL), c=mate))
        for k in range(NZL)
    ]
    for copy in sx_copies:
        copy.wait_recv()
    s = summed(sx_buf[x], lambda k: sx_in[k], NX - 1)
    out_ref[c, zh], out_ref[c, 1 - zh] = s[:NY], s[NY:]
    for copy in sz_copies:
        copy.wait_recv()
    s = summed(sz_in[0], lambda k: sz_in[k + 1], NZL - 1)
    out_ref[mate, zh], out_ref[mate, 1 - zh] = s[:NY], s[NY:]

    for copy in copies:
        copy.wait_send()


def shards(valence, conduction, points, inverse_metric):
    rows, width = valence.shape
    count = points.shape[0]
    piece = count // 2 // NY
    lines = NX * NZL * NY
    out = pl.pallas_call(
        kernel,
        out_shape=jax.ShapeDtypeStruct((2, 2, NY, width), F32),
        in_specs=[pl.BlockSpec(memory_space=pltpu.HBM)] * 4,
        out_specs=pl.BlockSpec(memory_space=pltpu.VMEM),
        scratch_shapes=[
            pltpu.VMEM((1, count), jnp.int32),
            pltpu.VMEM((rows, width), BF16),
            pltpu.VMEM((rows, width), BF16),
            pltpu.VMEM((count, width), BF16),
            pltpu.VMEM((rows, width), BF16),
            pltpu.VMEM((rows, width), BF16),
            pltpu.VMEM((count, width), BF16),
            pltpu.VMEM((NY, 1, 2 * width), F32),
            pltpu.VMEM((NZL, NY, 2 * width), F32),
            pltpu.VMEM((NX, 2, NZL * NY // 2, 2 * width), BF16),
            pltpu.VMEM((2, NY, piece, width), BF16),
            pltpu.VMEM((2, NY - 1, piece, width), BF16),
            pltpu.VMEM((2, piece, width), BF16),
            pltpu.VMEM((2, 3, piece, width), BF16),
            pltpu.VMEM((2, 2, NY, piece, lines), BF16),
            pltpu.VMEM((NX, 2, NZL * NY, width), BF16),
            pltpu.VMEM((NX - 1, 2, NZL * NY, width), BF16),
            pltpu.VMEM((NZL, 2, NX * NY, width), BF16),
            pltpu.VMEM((NZL - 1, 2, NX * NY, width), BF16),
            pltpu.VMEM((NX, 2 * NY, width), BF16),
            pltpu.VMEM((NX - 1, 2 * NY, width), BF16),
            pltpu.VMEM((NZL, 2 * NY, width), BF16),
            pltpu.VMEM((NZL, 2 * NY, width), BF16),
            pltpu.SemaphoreType.DMA((COPIES,)),
            pltpu.SemaphoreType.DMA((COPIES,)),
            pltpu.SemaphoreType.DMA((4,)),
        ],
        compiler_params=pltpu.CompilerParams(
            collective_id=0, has_side_effects=True, vmem_limit_bytes=63 * 2**20
        ),
    )(points[None, :], valence, conduction, inverse_metric)
    return out.transpose(2, 1, 0, 3).reshape(NY * 4, width).astype(BF16)


def solution(mesh):
    return jax.shard_map(
        shards,
        mesh=mesh,
        in_specs=(
            P(("grid", "interp"), None),
            P(("grid", "interp"), None),
            P("grid"),
            P("grid", "interp"),
        ),
        out_specs=P("grid", "interp"),
        check_vma=False,
    )
```

```python
import jax
import jax.numpy as jnp
from jax import lax
from jax.experimental import pallas as pl
from jax.experimental.pallas import tpu as pltpu
from jax.sharding import PartitionSpec as P

MESH = pl.DeviceIdType.MESH
BF16, F32 = jnp.bfloat16, jnp.float32

NX, NZL, NY = 8, 4, 8
COPIES = 112


def kernel(
    pts_hbm, val_hbm, con_hbm, met_hbm, out_ref,
    pts_ref, val_ref, con_ref, met_ref, val_mate, con_mate, met_mate, row_buf, zl_buf, blk_buf,
    pick_buf, pick_in, pick_z, pts_buf, pair_buf,
    part_buf, px_buf, px_in, pz_buf, pz_in, lx_buf, lx_in, lz_buf, lz_in, sx_buf, sx_in, sz_buf, sz_in,
    send_sem, recv_sem, load_sem, rest_send, rest_recv,
):
    g, i = lax.axis_index("grid"), lax.axis_index("interp")
    x, zl = lax.div(g, NZL), lax.rem(g, NZL)
    y, zh, c = lax.div(i, 4), lax.rem(lax.div(i, 2), 2), lax.rem(i, 2)
    rows, width = val_ref.shape
    half = pts_ref.shape[1] // 2
    piece = half // NY
    lines = NX * NZL * NY
    mate = 1 - c

    def device(x=x, zl=zl, y=y, zh=zh, c=c):
        return (x * NZL + zl, y * 4 + zh * 2 + c)

    y_peers = [device(y=lax.rem(y + k, NY)) for k in range(1, NY)]
    x_peers = [device(x=lax.rem(x + k, NX)) for k in range(1, NX)]
    zl_peers = [device(zl=lax.rem(zl + k, NZL)) for k in range(1, NZL)]
    zl_mates = [device(zl=lax.rem(zl + k, NZL), c=mate) for k in range(1, NZL)]
    z_peer, core_peer = device(zh=1 - zh), device(c=mate)

    barrier = pltpu.get_barrier_semaphore()
    peers = [core_peer, z_peer] + x_peers + y_peers + zl_peers + zl_mates
    for peer in peers:
        pl.semaphore_signal(barrier, inc=1, device_id=peer, device_id_type=MESH)

    loads = [
        pltpu.make_async_copy(src, dst, load_sem.at[n])
        for n, (src, dst) in enumerate(
            [(val_hbm, val_ref), (con_hbm, con_ref), (pts_hbm, pts_ref), (met_hbm, met_ref)]
        )
    ]
    for load in loads:
        load.start()

    copies = []

    def send(src, dst, peer):
        n = len(copies)
        copy = pltpu.make_async_remote_copy(
            src_ref=src,
            dst_ref=dst,
            send_sem=send_sem.at[n],
            recv_sem=recv_sem.at[n],
            device_id=peer,
            device_id_type=MESH,
        )
        copy.start()
        copies.append(copy)
        return copy

    for load in loads[:2]:
        load.wait()
    row_buf[y] = jnp.concatenate([val_ref[0:1, :], con_ref[0:1, :]], axis=1).astype(F32)

    pl.semaphore_wait(barrier, len(peers))

    row_copies = [send(row_buf.at[y], row_buf.at[y], peer) for peer in y_peers]
    core_rows = [send(val_ref, val_mate, core_peer), send(con_ref, con_mate, core_peer)]

    loads[2].wait()
    pts = pts_ref[:, pl.ds(pl.multiple_of(c * half, half), half)]
    spread = jnp.broadcast_to(pts, (128, half)).T

    def one_hot(owner):
        local = spread - owner * rows
        lane = lax.broadcasted_iota(jnp.int32, (half, 128), 1)
        return jnp.concatenate(
            [jnp.where(local == lane + at, 1.0, 0.0) for at in range(0, rows, 128)], axis=1
        ).astype(BF16)

    def picked(hot, ref):
        pick = jnp.dot(hot, ref[...], preferred_element_type=F32)
        return pick.astype(BF16).reshape(NY, 2, piece // 2, width)

    own = g * (NY * 4) + i
    hot, hot_mate = one_hot(own), one_hot(own - c + mate)

    sides = (slice(0, width), slice(width, 2 * width))
    picks = [picked(hot, ref) for ref in (val_ref, con_ref)]
    for n, ref in enumerate((val_mate, con_mate)):
        core_rows[n].wait_recv()
        pick = picks[n] + picked(hot_mate, ref)
        for h in range(2):
            pick_buf[h, :, :, sides[n]] = pick[:, h]
    pick_copies = [
        [
            send(pick_buf.at[h, lax.rem(y + k, NY)], pick_in.at[h, k - 1], y_peers[k - 1])
            for k in range(1, NY)
        ]
        for h in range(2)
    ]

    for copy in row_copies:
        copy.wait_recv()
    for k in range(NY):
        zl_buf[zl, k : k + 1, :] = row_buf[k]
    zl_copies = [send(zl_buf.at[zl], zl_buf.at[zl], peer) for peer in zl_peers]

    for copy in zl_copies:
        copy.wait_recv()
    blk_buf[x] = zl_buf[...].reshape(2, NZL * NY // 2, 2 * width).astype(BF16)
    blk_copies = [send(blk_buf.at[x], blk_buf.at[x], peer) for peer in x_peers]
    loads[3].wait()
    core_met = send(met_ref, met_mate, core_peer)

    z_copies = []
    for h in range(2):
        for copy in pick_copies[h]:
            copy.wait_recv()
        total = pick_buf[h, y].astype(F32)
        for k in range(NY - 1):
            total += pick_in[h, k].astype(F32)
        pts_buf[h, 0] = total.astype(BF16)
        z_copies.append(send(pts_buf.at[h, 0], pick_z.at[h], z_peer))
    across = (((1,), (1,)), ((), ()))
    pair_z, pair_copies = [], [[], []]
    for h in range(2):
        z_copies[h].wait_recv()
        pts_buf[h, 1 + c] = (pts_buf[h, 0].astype(F32) + pick_z[h].astype(F32)).astype(BF16)
        core_copy = send(pts_buf.at[h, 1 + c], pts_buf.at[h, 1 + c], core_peer)
        if h == 0:
            for copy in blk_copies:
                copy.wait_recv()
        core_copy.wait_recv()
        points = pts_buf[h, 1:].reshape(piece, 2 * width)
        grams = [
            lax.dot_general(
                points[:, side], blk_buf[...].reshape(lines, 2 * width)[:, side], across,
                preferred_element_type=F32,
            )
            for side in sides
        ]
        pair = (grams[0] * grams[1]).astype(BF16)
        pair_buf[0, :, y, h] = pair.reshape(2, piece // 2, lines)
        mine, theirs = pair_buf.at[0, :, y, h], pair_buf.at[1, :, y, h]
        pair_z.append(send(mine, theirs, z_peer))
        pair_copies[0] += [send(mine, mine, peer) for peer in y_peers]
    for h in range(2):
        pair_z[h].wait_recv()
        theirs = pair_buf.at[1, :, y, h]
        pair_copies[1] += [send(theirs, theirs, peer) for peer in y_peers]
    core_met.wait_recv()

    down = (((0,), (0,)), ((), ()))
    i_mate = i - c + mate
    x_from, zl_from = lax.div(i_mate, NZL), lax.rem(i, NZL)
    x_line = (lax.rem(i_mate, NZL) == zl) & (x_from < NX)
    zl_line = lax.div(i, NZL) == x
    rest_x = dict(
        n=0, src=x_line & (x_from == x), dst=x_line & (x_from != x), peers=x_peers, pos=x, size=NX,
        hold=lx_buf, inbox=lx_in,
    )
    rest_z = dict(
        n=1, src=zl_line & (zl_from == zl), dst=zl_line & (zl_from != zl), peers=zl_peers, pos=zl, size=NZL,
        hold=lz_buf, inbox=lz_in,
    )

    def rest_copy(rest, q, k):
        return pltpu.make_async_remote_copy(
            src_ref=rest["hold"].at[q, lax.rem(rest["pos"] + k, rest["size"])],
            dst_ref=rest["inbox"].at[q],
            send_sem=rest_send.at[rest["n"], q, k - 1],
            recv_sem=rest_recv.at[rest["n"], q],
            device_id=rest["peers"][k - 1],
            device_id_type=MESH,
        )

    def send_rest(rest, q):
        for k in range(1, rest["size"]):
            rest_copy(rest, q, k).start()

    def add_rest(rest, q, total):
        @pl.when(rest["src"])
        def _():
            total[q] += rest["hold"][q, rest["pos"]].astype(F32).reshape(total.shape[1:])

        if rest["size"] > 1:

            @pl.when(rest["dst"])
            def _():
                rest_copy(rest, q, 1).wait_recv()
                total[q] += rest["inbox"][q].astype(F32).reshape(total.shape[1:])

    px_copies, pz_copies = [], []
    for q in range(2):
        for copy in pair_copies[q]:
            copy.wait_recv()
        pair_q = pair_buf[q].reshape(2 * half, lines)
        part_buf[...] = lax.dot_general(pair_q, met_mate[...], down, preferred_element_type=F32)
        px_buf[q] = part_buf[...].astype(BF16).reshape(NX, NZL * NY, width)
        px_copies.append([
            send(px_buf.at[q, lax.rem(x + k, NX)], px_in.at[q, k - 1], x_peers[k - 1])
            for k in range(1, NX)
        ])

        @pl.when(rest_x["src"])
        def _():
            part = part_buf[...].reshape(NX, NZL * NY, width)
            lx_buf[q] = (part - px_buf[q].astype(F32)).astype(BF16)
            send_rest(rest_x, q)

        part_buf[...] = lax.dot_general(pair_q, met_ref[...], down, preferred_element_type=F32)
        for k in range(NZL):
            part = part_buf[...].reshape(NX, NZL, NY, width)[:, k]
            pz_buf[q, k] = part.reshape(NX * NY, width).astype(BF16)
        pz_copies.append([
            send(pz_buf.at[q, lax.rem(zl + k, NZL)], pz_in.at[q, k - 1], zl_peers[k - 1])
            for k in range(1, NZL)
        ])

        @pl.when(rest_z["src"])
        def _():
            for k in range(NZL):
                part = part_buf[...].reshape(NX, NZL, NY, width)[:, k].reshape(NX * NY, width)
                lz_buf[q, k] = (part - pz_buf[q, k].astype(F32)).astype(BF16)
            send_rest(rest_z, q)

    def summed(own, inbox, count):
        total = own.astype(F32)
        for k in range(count):
            total += inbox(k).astype(F32)
        return total

    for q in range(2):
        for copy in pz_copies[q]:
            copy.wait_recv()
        total = summed(pz_buf[q, zl], lambda k: pz_in[q, k], NZL - 1)
        sx_buf[q] = total.reshape(NX, NY, width)
        add_rest(rest_z, q, sx_buf)
        if q == 1:
            sx_copies = [
                send(sx_buf.at[:, lax.rem(x + k, NX)], sx_in.at[k - 1], x_peers[k - 1])
                for k in range(1, NX)
            ]
        for copy in px_copies[q]:
            copy.wait_recv()
        total = summed(px_buf[q, x], lambda k: px_in[q, k], NX - 1)
        sz_buf[q] = total.reshape(NZL, NY, width)
        add_rest(rest_x, q, sz_buf)
    sz_copies = []
    for k in range(NZL):
        to_zl = lax.rem(zl + k, NZL)
        sz_copies.append(send(sz_buf.at[:, to_zl], sz_in.at[k], device(zl=to_zl, c=mate)))
    for copy in sx_copies:
        copy.wait_recv()
    total = summed(sx_buf[:, x], lambda k: sx_in[k], NX - 1)
    out_ref[c, zh], out_ref[c, 1 - zh] = total[0], total[1]
    for copy in sz_copies:
        copy.wait_recv()
    total = summed(sz_in[0], lambda k: sz_in[k + 1], NZL - 1)
    out_ref[mate, zh], out_ref[mate, 1 - zh] = total[0], total[1]

    for rest in (rest_x, rest_z):

        @pl.when(rest["src"])
        def _():
            for q in range(2):
                for k in range(1, rest["size"]):
                    rest_copy(rest, q, k).wait_send()

    for copy in copies:
        copy.wait_send()


def shards(valence, conduction, points, inverse_metric):
    rows, width = valence.shape
    count = points.shape[0]
    piece = count // 2 // NY
    lines = NX * NZL * NY
    out = pl.pallas_call(
        kernel,
        out_shape=jax.ShapeDtypeStruct((2, 2, NY, width), F32),
        in_specs=[pl.BlockSpec(memory_space=pltpu.HBM)] * 4,
        out_specs=pl.BlockSpec(memory_space=pltpu.VMEM),
        scratch_shapes=[
            pltpu.VMEM((1, count), jnp.int32),
            pltpu.VMEM((rows, width), BF16),
            pltpu.VMEM((rows, width), BF16),
            pltpu.VMEM((count, width), BF16),
            pltpu.VMEM((rows, width), BF16),
            pltpu.VMEM((rows, width), BF16),
            pltpu.VMEM((count, width), BF16),
            pltpu.VMEM((NY, 1, 2 * width), F32),
            pltpu.VMEM((NZL, NY, 2 * width), F32),
            pltpu.VMEM((NX, 2, NZL * NY // 2, 2 * width), BF16),
            pltpu.VMEM((2, NY, piece // 2, 2 * width), BF16),
            pltpu.VMEM((2, NY - 1, piece // 2, 2 * width), BF16),
            pltpu.VMEM((2, piece // 2, 2 * width), BF16),
            pltpu.VMEM((2, 3, piece // 2, 2 * width), BF16),
            pltpu.VMEM((2, 2, NY, 2, piece // 2, lines), BF16),
            pltpu.VMEM((lines, width), F32),
            pltpu.VMEM((2, NX, NZL * NY, width), BF16),
            pltpu.VMEM((2, NX - 1, NZL * NY, width), BF16),
            pltpu.VMEM((2, NZL, NX * NY, width), BF16),
            pltpu.VMEM((2, NZL - 1, NX * NY, width), BF16),
            pltpu.VMEM((2, NX, NZL * NY, width), BF16),
            pltpu.VMEM((2, NZL * NY, width), BF16),
            pltpu.VMEM((2, NZL, NX * NY, width), BF16),
            pltpu.VMEM((2, NX * NY, width), BF16),
            pltpu.VMEM((2, NX, NY, width), F32),
            pltpu.VMEM((NX - 1, 2, NY, width), F32),
            pltpu.VMEM((2, NZL, NY, width), F32),
            pltpu.VMEM((NZL, 2, NY, width), F32),
            pltpu.SemaphoreType.DMA((COPIES,)),
            pltpu.SemaphoreType.DMA((COPIES,)),
            pltpu.SemaphoreType.DMA((4,)),
            pltpu.SemaphoreType.DMA((2, 2, NX - 1)),
            pltpu.SemaphoreType.DMA((2, 2)),
        ],
        compiler_params=pltpu.CompilerParams(
            collective_id=0, has_side_effects=True, vmem_limit_bytes=63 * 2**20
        ),
    )(points[None, :], valence, conduction, inverse_metric)
    return out.transpose(2, 1, 0, 3).reshape(NY * 4, width).astype(BF16)


def solution(mesh):
    return jax.shard_map(
        shards,
        mesh=mesh,
        in_specs=(
            P(("grid", "interp"), None),
            P(("grid", "interp"), None),
            P("grid"),
            P("grid", "interp"),
        ),
        out_specs=P("grid", "interp"),
        check_vma=False,
    )
```

```python
import jax
import jax.numpy as jnp
from jax import lax
from jax.experimental import pallas as pl
from jax.experimental.pallas import tpu as pltpu
from jax.sharding import PartitionSpec as P

MESH = pl.DeviceIdType.MESH
BF16, F32 = jnp.bfloat16, jnp.float32

NX, NZL, NY = 8, 4, 8
COPIES = 112


def kernel(
    pts_hbm, val_hbm, con_hbm, met_hbm, out_ref,
    pts_ref, val_ref, con_ref, met_ref, val_mate, con_mate, met_mate, row_buf, zl_buf, blk_buf,
    pick_buf, pick_in, pick_z, pts_buf, pair_buf,
    part_buf, px_buf, px_in, pz_buf, pz_in, low_part, low_in, sx_buf, sx_in, sz_buf, sz_in,
    send_sem, recv_sem, load_sem, low_send, low_recv,
):
    g, i = lax.axis_index("grid"), lax.axis_index("interp")
    x, zl = lax.div(g, NZL), lax.rem(g, NZL)
    y, zh, c = lax.div(i, 4), lax.rem(lax.div(i, 2), 2), lax.rem(i, 2)
    rows, width = val_ref.shape
    half = pts_ref.shape[1] // 2
    piece = half // NY
    lines = NX * NZL * NY
    mate = 1 - c

    def device(x=x, zl=zl, y=y, zh=zh, c=c):
        return (x * NZL + zl, y * 4 + zh * 2 + c)

    y_peers = [device(y=lax.rem(y + k, NY)) for k in range(1, NY)]
    x_peers = [device(x=lax.rem(x + k, NX)) for k in range(1, NX)]
    zl_peers = [device(zl=lax.rem(zl + k, NZL)) for k in range(1, NZL)]
    zl_mates = [device(zl=lax.rem(zl + k, NZL), c=mate) for k in range(1, NZL)]
    z_peer, core_peer = device(zh=1 - zh), device(c=mate)

    barrier = pltpu.get_barrier_semaphore()
    peers = [core_peer, z_peer] + x_peers + y_peers + zl_peers + zl_mates
    for peer in peers:
        pl.semaphore_signal(barrier, inc=1, device_id=peer, device_id_type=MESH)

    loads = [
        pltpu.make_async_copy(src, dst, load_sem.at[n])
        for n, (src, dst) in enumerate(
            [(val_hbm, val_ref), (con_hbm, con_ref), (pts_hbm, pts_ref), (met_hbm, met_ref)]
        )
    ]
    for load in loads:
        load.start()

    copies = []

    def send(src, dst, peer):
        n = len(copies)
        copy = pltpu.make_async_remote_copy(
            src_ref=src,
            dst_ref=dst,
            send_sem=send_sem.at[n],
            recv_sem=recv_sem.at[n],
            device_id=peer,
            device_id_type=MESH,
        )
        copy.start()
        copies.append(copy)
        return copy

    for load in loads[:2]:
        load.wait()
    row_buf[y] = jnp.concatenate([val_ref[0:1, :], con_ref[0:1, :]], axis=1).astype(F32)

    pl.semaphore_wait(barrier, len(peers))

    row_copies = [send(row_buf.at[y], row_buf.at[y], peer) for peer in y_peers]
    core_rows = [send(val_ref, val_mate, core_peer), send(con_ref, con_mate, core_peer)]

    loads[2].wait()
    pts = pts_ref[:, pl.ds(pl.multiple_of(c * half, half), half)]
    spread = jnp.broadcast_to(pts, (128, half)).T

    def one_hot(owner):
        local = spread - owner * rows
        lane = lax.broadcasted_iota(jnp.int32, (half, 128), 1)
        return jnp.concatenate(
            [jnp.where(local == lane + at, 1.0, 0.0) for at in range(0, rows, 128)], axis=1
        ).astype(BF16)

    def picked(hot, ref):
        pick = jnp.dot(hot, ref[...], preferred_element_type=F32)
        return pick.astype(BF16).reshape(NY, 2, piece // 2, width)

    own = g * (NY * 4) + i
    hot, hot_mate = one_hot(own), one_hot(own - c + mate)

    sides = (slice(0, width), slice(width, 2 * width))
    picks = [picked(hot, ref) for ref in (val_ref, con_ref)]
    for n, ref in enumerate((val_mate, con_mate)):
        core_rows[n].wait_recv()
        pick = picks[n] + picked(hot_mate, ref)
        for h in range(2):
            pick_buf[h, :, :, sides[n]] = pick[:, h]
    pick_copies = [
        [
            send(pick_buf.at[h, lax.rem(y + k, NY)], pick_in.at[h, k - 1], y_peers[k - 1])
            for k in range(1, NY)
        ]
        for h in range(2)
    ]

    for copy in row_copies:
        copy.wait_recv()
    for k in range(NY):
        zl_buf[zl, k : k + 1, :] = row_buf[k]
    zl_copies = [send(zl_buf.at[zl], zl_buf.at[zl], peer) for peer in zl_peers]

    for copy in zl_copies:
        copy.wait_recv()
    blk_buf[x] = zl_buf[...].reshape(2, NZL * NY // 2, 2 * width).astype(BF16)
    blk_copies = [send(blk_buf.at[x], blk_buf.at[x], peer) for peer in x_peers]
    loads[3].wait()
    core_met = send(met_ref, met_mate, core_peer)

    z_copies = []
    for h in range(2):
        for copy in pick_copies[h]:
            copy.wait_recv()
        total = pick_buf[h, y].astype(F32)
        for k in range(NY - 1):
            total += pick_in[h, k].astype(F32)
        pts_buf[h, 0] = total.astype(BF16)
        z_copies.append(send(pts_buf.at[h, 0], pick_z.at[h], z_peer))
    across = (((1,), (1,)), ((), ()))
    pair_z, pair_copies = [], [[], []]
    for h in range(2):
        z_copies[h].wait_recv()
        pts_buf[h, 1 + c] = (pts_buf[h, 0].astype(F32) + pick_z[h].astype(F32)).astype(BF16)
        core_copy = send(pts_buf.at[h, 1 + c], pts_buf.at[h, 1 + c], core_peer)
        if h == 0:
            for copy in blk_copies:
                copy.wait_recv()
        core_copy.wait_recv()
        points = pts_buf[h, 1:].reshape(piece, 2 * width)
        grams = [
            lax.dot_general(
                points[:, side], blk_buf[...].reshape(lines, 2 * width)[:, side], across,
                preferred_element_type=F32,
            )
            for side in sides
        ]
        pair = (grams[0] * grams[1]).astype(BF16)
        pair_buf[0, :, y, h] = pair.reshape(2, piece // 2, lines)
        mine, theirs = pair_buf.at[0, :, y, h], pair_buf.at[1, :, y, h]
        pair_z.append(send(mine, theirs, z_peer))
        pair_copies[0] += [send(mine, mine, peer) for peer in y_peers]
    for h in range(2):
        pair_z[h].wait_recv()
        theirs = pair_buf.at[1, :, y, h]
        pair_copies[1] += [send(theirs, theirs, peer) for peer in y_peers]
    core_met.wait_recv()

    down = (((0,), (0,)), ((), ()))
    lead, lead_mate = g == i, g == i - c + mate
    side = width // 2

    def low_copy(role, q, kx, kz):
        to_x, to_zl = lax.rem(x + kx, NX), lax.rem(zl + kz, NZL)
        return pltpu.make_async_remote_copy(
            src_ref=low_part.at[q, to_x, to_zl],
            dst_ref=low_in.at[role, q],
            send_sem=low_send.at[q, kx * NZL + kz],
            recv_sem=low_recv.at[role, q],
            device_id=device(x=to_x, zl=to_zl, c=mate if role else c),
            device_id_type=MESH,
        )

    def low_copies(role, q):
        at = [(kx, kz) for kx in range(NX) for kz in range(NZL) if kx or kz or role]
        return [low_copy(role, q, kx, kz) for kx, kz in at]

    def keep_low(q, rounded):
        part = part_buf[...].reshape(NX, NZL, NY, width)
        low = part - rounded
        low = jnp.concatenate([low[..., :side], low[..., side:]], axis=2)
        low_part[q] = low.astype(BF16)

    def low_rows(low):
        low = low.astype(F32)
        return jnp.concatenate([low[:NY], low[NY:]], axis=1)

    px_copies, pz_copies = [], []
    for q in range(2):
        for copy in pair_copies[q]:
            copy.wait_recv()
        pair_q = pair_buf[q].reshape(2 * half, lines)
        part_buf[...] = lax.dot_general(pair_q, met_mate[...], down, preferred_element_type=F32)
        px_buf[q] = part_buf[...].astype(BF16).reshape(NX, NZL * NY, width)
        px_copies.append([
            send(px_buf.at[q, lax.rem(x + k, NX)], px_in.at[q, k - 1], x_peers[k - 1])
            for k in range(1, NX)
        ])

        @pl.when(lead_mate)
        def _():
            keep_low(q, px_buf[q].astype(F32).reshape(NX, NZL, NY, width))

        part_buf[...] = lax.dot_general(pair_q, met_ref[...], down, preferred_element_type=F32)
        for k in range(NZL):
            part = part_buf[...].reshape(NX, NZL, NY, width)[:, k]
            pz_buf[q, k] = part.reshape(NX * NY, width).astype(BF16)
        pz_copies.append([
            send(pz_buf.at[q, lax.rem(zl + k, NZL)], pz_in.at[q, k - 1], zl_peers[k - 1])
            for k in range(1, NZL)
        ])

        @pl.when(lead)
        def _():
            part = part_buf[...]
            keep_low(q, part.astype(BF16).astype(F32).reshape(NX, NZL, NY, width))

        for role, leads in enumerate((lead, lead_mate)):

            @pl.when(leads)
            def _():
                for copy in low_copies(role, q):
                    copy.start()

    def summed(own, inbox, count):
        total = own.astype(F32)
        for k in range(count):
            total += inbox(k).astype(F32)
        return total

    for q in range(2):
        for copy in pz_copies[q]:
            copy.wait_recv()
        total = summed(pz_buf[q, zl], lambda k: pz_in[q, k], NZL - 1)
        sx_buf[q] = total.reshape(NX, NY, width)
        if q == 1:
            sx_copies = [
                send(sx_buf.at[:, lax.rem(x + k, NX)], sx_in.at[k - 1], x_peers[k - 1])
                for k in range(1, NX)
            ]
        for copy in px_copies[q]:
            copy.wait_recv()
        total = summed(px_buf[q, x], lambda k: px_in[q, k], NX - 1)
        sz_buf[q] = total.reshape(NZL, NY, width)
    sz_copies = []
    for k in range(NZL):
        to_zl = lax.rem(zl + k, NZL)
        sz_copies.append(send(sz_buf.at[:, to_zl], sz_in.at[k], device(zl=to_zl, c=mate)))
    halves = ((0, zh), (1, 1 - zh))
    for copy in sx_copies:
        copy.wait_recv()
    total = summed(sx_buf[:, x], lambda k: sx_in[k], NX - 1)
    for q, at in halves:
        out_ref[c, at] = total[q]

    @pl.when(lead)
    def _():
        for q, at in halves:
            out_ref[c, at] += low_rows(low_part[q, x, zl])

    @pl.when(jnp.logical_not(lead))
    def _():
        for q, at in halves:
            low_copy(0, q, 1, 0).wait_recv()
            out_ref[c, at] += low_rows(low_in[0, q])

    for copy in sz_copies:
        copy.wait_recv()
    total = summed(sz_in[0], lambda k: sz_in[k + 1], NZL - 1)
    for q, at in halves:
        low_copy(1, q, 1, 0).wait_recv()
        out_ref[mate, at] = total[q] + low_rows(low_in[1, q])

    for copy in copies:
        copy.wait_send()
    for role, leads in enumerate((lead, lead_mate)):

        @pl.when(leads)
        def _():
            for q in range(2):
                for copy in low_copies(role, q):
                    copy.wait_send()


def shards(valence, conduction, points, inverse_metric):
    rows, width = valence.shape
    count = points.shape[0]
    piece = count // 2 // NY
    lines = NX * NZL * NY
    out = pl.pallas_call(
        kernel,
        out_shape=jax.ShapeDtypeStruct((2, 2, NY, width), F32),
        in_specs=[pl.BlockSpec(memory_space=pltpu.HBM)] * 4,
        out_specs=pl.BlockSpec(memory_space=pltpu.VMEM),
        scratch_shapes=[
            pltpu.VMEM((1, count), jnp.int32),
            pltpu.VMEM((rows, width), BF16),
            pltpu.VMEM((rows, width), BF16),
            pltpu.VMEM((count, width), BF16),
            pltpu.VMEM((rows, width), BF16),
            pltpu.VMEM((rows, width), BF16),
            pltpu.VMEM((count, width), BF16),
            pltpu.VMEM((NY, 1, 2 * width), F32),
            pltpu.VMEM((NZL, NY, 2 * width), F32),
            pltpu.VMEM((NX, 2, NZL * NY // 2, 2 * width), BF16),
            pltpu.VMEM((2, NY, piece // 2, 2 * width), BF16),
            pltpu.VMEM((2, NY - 1, piece // 2, 2 * width), BF16),
            pltpu.VMEM((2, piece // 2, 2 * width), BF16),
            pltpu.VMEM((2, 3, piece // 2, 2 * width), BF16),
            pltpu.VMEM((2, 2, NY, 2, piece // 2, lines), BF16),
            pltpu.VMEM((lines, width), F32),
            pltpu.VMEM((2, NX, NZL * NY, width), BF16),
            pltpu.VMEM((2, NX - 1, NZL * NY, width), BF16),
            pltpu.VMEM((2, NZL, NX * NY, width), BF16),
            pltpu.VMEM((2, NZL - 1, NX * NY, width), BF16),
            pltpu.VMEM((2, NX, NZL, 2 * NY, width // 2), BF16),
            pltpu.VMEM((2, 2, 2 * NY, width // 2), BF16),
            pltpu.VMEM((2, NX, NY, width), F32),
            pltpu.VMEM((NX - 1, 2, NY, width), F32),
            pltpu.VMEM((2, NZL, NY, width), F32),
            pltpu.VMEM((NZL, 2, NY, width), F32),
            pltpu.SemaphoreType.DMA((COPIES,)),
            pltpu.SemaphoreType.DMA((COPIES,)),
            pltpu.SemaphoreType.DMA((4,)),
            pltpu.SemaphoreType.DMA((2, NX * NZL)),
            pltpu.SemaphoreType.DMA((2, 2)),
        ],
        compiler_params=pltpu.CompilerParams(
            collective_id=0, has_side_effects=True, vmem_limit_bytes=63 * 2**20
        ),
    )(points[None, :], valence, conduction, inverse_metric)
    return out.transpose(2, 1, 0, 3).reshape(NY * 4, width).astype(BF16)


def solution(mesh):
    return jax.shard_map(
        shards,
        mesh=mesh,
        in_specs=(
            P(("grid", "interp"), None),
            P(("grid", "interp"), None),
            P("grid"),
            P("grid", "interp"),
        ),
        out_specs=P("grid", "interp"),
        check_vma=False,
    )
```

```python
import jax
import jax.numpy as jnp
from jax import lax
from jax.experimental import pallas as pl
from jax.experimental.pallas import tpu as pltpu
from jax.sharding import PartitionSpec as P

MESH = pl.DeviceIdType.MESH
BF16, F32 = jnp.bfloat16, jnp.float32

NX, NZL, NY = 8, 4, 8
COPIES = 112


def kernel(
    pts_hbm, val_hbm, con_hbm, met_hbm, out_ref,
    pts_ref, val_ref, con_ref, met_ref, val_mate, con_mate, met_mate, row_buf, zl_buf, blk_buf,
    pick_buf, pick_in, pick_z, pts_buf, pair_buf,
    part_buf, px_buf, px_in, pz_buf, pz_in, low_part, low_in, sx_buf, sx_in, sz_buf, sz_in,
    send_sem, recv_sem, load_sem, low_send, low_recv,
):
    g, i = lax.axis_index("grid"), lax.axis_index("interp")
    x, zl = lax.div(g, NZL), lax.rem(g, NZL)
    y, zh, c = lax.div(i, 4), lax.rem(lax.div(i, 2), 2), lax.rem(i, 2)
    rows, width = val_ref.shape
    half = pts_ref.shape[1] // 2
    piece = half // NY
    lines = NX * NZL * NY
    mate = 1 - c

    def device(x=x, zl=zl, y=y, zh=zh, c=c):
        return (x * NZL + zl, y * 4 + zh * 2 + c)

    y_peers = [device(y=lax.rem(y + k, NY)) for k in range(1, NY)]
    x_peers = [device(x=lax.rem(x + k, NX)) for k in range(1, NX)]
    zl_peers = [device(zl=lax.rem(zl + k, NZL)) for k in range(1, NZL)]
    zl_mates = [device(zl=lax.rem(zl + k, NZL), c=mate) for k in range(1, NZL)]
    z_peer, core_peer = device(zh=1 - zh), device(c=mate)

    barrier = pltpu.get_barrier_semaphore()
    peers = [core_peer, z_peer] + x_peers + y_peers + zl_peers + zl_mates
    for peer in peers:
        pl.semaphore_signal(barrier, inc=1, device_id=peer, device_id_type=MESH)

    loads = [
        pltpu.make_async_copy(src, dst, load_sem.at[n])
        for n, (src, dst) in enumerate(
            [(val_hbm, val_ref), (con_hbm, con_ref), (pts_hbm, pts_ref), (met_hbm, met_ref)]
        )
    ]
    for load in loads:
        load.start()

    copies = []

    def send(src, dst, peer):
        n = len(copies)
        copy = pltpu.make_async_remote_copy(
            src_ref=src,
            dst_ref=dst,
            send_sem=send_sem.at[n],
            recv_sem=recv_sem.at[n],
            device_id=peer,
            device_id_type=MESH,
        )
        copy.start()
        copies.append(copy)
        return copy

    for load in loads[:2]:
        load.wait()
    row_buf[y] = jnp.concatenate([val_ref[0:1, :], con_ref[0:1, :]], axis=1).astype(F32)

    pl.semaphore_wait(barrier, len(peers))

    row_copies = [send(row_buf.at[y], row_buf.at[y], peer) for peer in y_peers]
    core_rows = [send(val_ref, val_mate, core_peer), send(con_ref, con_mate, core_peer)]

    loads[2].wait()
    pts = pts_ref[:, pl.ds(pl.multiple_of(c * half, half), half)]
    spread = jnp.broadcast_to(pts, (128, half)).T

    def one_hot(owner):
        local = spread - owner * rows
        lane = lax.broadcasted_iota(jnp.int32, (half, 128), 1)
        return jnp.concatenate(
            [jnp.where(local == lane + at, 1.0, 0.0) for at in range(0, rows, 128)], axis=1
        ).astype(BF16)

    def picked(hot, ref):
        pick = jnp.dot(hot, ref[...], preferred_element_type=F32)
        return pick.astype(BF16).reshape(NY, 2, piece // 2, width)

    own = g * (NY * 4) + i
    hot, hot_mate = one_hot(own), one_hot(own - c + mate)

    sides = (slice(0, width), slice(width, 2 * width))
    picks = [picked(hot, ref) for ref in (val_ref, con_ref)]
    for copy in row_copies:
        copy.wait_recv()
    for k in range(NY):
        zl_buf[zl, k : k + 1, :] = row_buf[k]
    zl_copies = [send(zl_buf.at[zl], zl_buf.at[zl], peer) for peer in zl_peers]
    for n, ref in enumerate((val_mate, con_mate)):
        core_rows[n].wait_recv()
        pick = picks[n] + picked(hot_mate, ref)
        for h in range(2):
            pick_buf[h, :, :, sides[n]] = pick[:, h]
    pick_copies = [
        [
            send(pick_buf.at[h, lax.rem(y + k, NY)], pick_in.at[h, k - 1], y_peers[k - 1])
            for k in range(1, NY)
        ]
        for h in range(2)
    ]

    for copy in zl_copies:
        copy.wait_recv()
    blk_buf[x] = zl_buf[...].reshape(2, NZL * NY // 2, 2 * width).astype(BF16)
    blk_copies = [send(blk_buf.at[x], blk_buf.at[x], peer) for peer in x_peers]
    loads[3].wait()
    core_met = send(met_ref, met_mate, core_peer)

    z_copies = []
    for h in range(2):
        for copy in pick_copies[h]:
            copy.wait_recv()
        total = pick_buf[h, y].astype(F32)
        for k in range(NY - 1):
            total += pick_in[h, k].astype(F32)
        pts_buf[h, 0] = total.astype(BF16)
        z_copies.append(send(pts_buf.at[h, 0], pick_z.at[h], z_peer))
    across = (((1,), (1,)), ((), ()))
    pair_z, pair_copies = [], [[], []]
    for h in range(2):
        z_copies[h].wait_recv()
        pts_buf[h, 1 + c] = (pts_buf[h, 0].astype(F32) + pick_z[h].astype(F32)).astype(BF16)
        core_copy = send(pts_buf.at[h, 1 + c], pts_buf.at[h, 1 + c], core_peer)
        if h == 0:
            for copy in blk_copies:
                copy.wait_recv()
        core_copy.wait_recv()
        points = pts_buf[h, 1:].reshape(piece, 2 * width)
        grams = [
            lax.dot_general(
                points[:, side], blk_buf[...].reshape(lines, 2 * width)[:, side], across,
                preferred_element_type=F32,
            )
            for side in sides
        ]
        pair = (grams[0] * grams[1]).astype(BF16)
        pair_buf[0, :, y, h] = pair.reshape(2, piece // 2, lines)
        mine, theirs = pair_buf.at[0, :, y, h], pair_buf.at[1, :, y, h]
        pair_z.append(send(mine, theirs, z_peer))
        pair_copies[0] += [send(mine, mine, peer) for peer in y_peers]
    for h in range(2):
        pair_z[h].wait_recv()
        theirs = pair_buf.at[1, :, y, h]
        pair_copies[1] += [send(theirs, theirs, peer) for peer in y_peers]
    core_met.wait_recv()

    down = (((0,), (0,)), ((), ()))
    lead, lead_mate = g == i, g == i - c + mate
    side = width // 2

    def low_copy(role, q, kx, kz):
        to_x, to_zl = lax.rem(x + kx, NX), lax.rem(zl + kz, NZL)
        return pltpu.make_async_remote_copy(
            src_ref=low_part.at[q, to_x, to_zl],
            dst_ref=low_in.at[role, q],
            send_sem=low_send.at[q, kx * NZL + kz],
            recv_sem=low_recv.at[role, q],
            device_id=device(x=to_x, zl=to_zl, c=mate if role else c),
            device_id_type=MESH,
        )

    def low_copies(role, q):
        at = [(kx, kz) for kx in range(NX) for kz in range(NZL) if kx or kz or role]
        return [low_copy(role, q, kx, kz) for kx, kz in at]

    def keep_low(q, rounded):
        part = part_buf[...].reshape(NX, NZL, NY, width)
        low = part - rounded
        low = jnp.concatenate([low[..., :side], low[..., side:]], axis=2)
        low_part[q] = low.astype(BF16)

    def low_rows(low):
        low = low.astype(F32)
        return jnp.concatenate([low[:NY], low[NY:]], axis=1)

    px_copies, pz_copies = [], []
    for q in range(2):
        for copy in pair_copies[q]:
            copy.wait_recv()
        pair_q = pair_buf[q].reshape(2 * half, lines)
        part_buf[...] = lax.dot_general(pair_q, met_mate[...], down, preferred_element_type=F32)
        px_buf[q] = part_buf[...].astype(BF16).reshape(NX, NZL * NY, width)
        px_copies.append([
            send(px_buf.at[q, lax.rem(x + k, NX)], px_in.at[q, k - 1], x_peers[k - 1])
            for k in range(1, NX)
        ])

        @pl.when(lead_mate)
        def _():
            keep_low(q, px_buf[q].astype(F32).reshape(NX, NZL, NY, width))

        part_buf[...] = lax.dot_general(pair_q, met_ref[...], down, preferred_element_type=F32)
        for k in range(NZL):
            part = part_buf[...].reshape(NX, NZL, NY, width)[:, k]
            pz_buf[q, k] = part.reshape(NX * NY, width).astype(BF16)
        pz_copies.append([
            send(pz_buf.at[q, lax.rem(zl + k, NZL)], pz_in.at[q, k - 1], zl_peers[k - 1])
            for k in range(1, NZL)
        ])

        @pl.when(lead)
        def _():
            part = part_buf[...]
            keep_low(q, part.astype(BF16).astype(F32).reshape(NX, NZL, NY, width))

        for role, leads in enumerate((lead, lead_mate)):

            @pl.when(leads)
            def _():
                for copy in low_copies(role, q):
                    copy.start()

    def summed(own, inbox, count):
        total = own.astype(F32)
        for k in range(count):
            total += inbox(k).astype(F32)
        return total

    for q in range(2):
        for copy in pz_copies[q]:
            copy.wait_recv()
        total = summed(pz_buf[q, zl], lambda k: pz_in[q, k], NZL - 1)
        sx_buf[q] = total.reshape(NX, NY, width)
        if q == 1:
            sx_copies = [
                send(sx_buf.at[:, lax.rem(x + k, NX)], sx_in.at[k - 1], x_peers[k - 1])
                for k in range(1, NX)
            ]
        for copy in px_copies[q]:
            copy.wait_recv()
        total = summed(px_buf[q, x], lambda k: px_in[q, k], NX - 1)
        sz_buf[q] = total.reshape(NZL, NY, width)
    sz_copies = []
    for k in range(NZL):
        to_zl = lax.rem(zl + k, NZL)
        sz_copies.append(send(sz_buf.at[:, to_zl], sz_in.at[k], device(zl=to_zl, c=mate)))
    halves = ((0, zh), (1, 1 - zh))
    for copy in sx_copies:
        copy.wait_recv()
    total = summed(sx_buf[:, x], lambda k: sx_in[k], NX - 1)
    for q, at in halves:
        out_ref[c, at] = total[q]

    @pl.when(lead)
    def _():
        for q, at in halves:
            out_ref[c, at] += low_rows(low_part[q, x, zl])

    @pl.when(jnp.logical_not(lead))
    def _():
        for q, at in halves:
            low_copy(0, q, 1, 0).wait_recv()
            out_ref[c, at] += low_rows(low_in[0, q])

    for copy in sz_copies:
        copy.wait_recv()
    total = summed(sz_in[0], lambda k: sz_in[k + 1], NZL - 1)
    for q, at in halves:
        low_copy(1, q, 1, 0).wait_recv()
        out_ref[mate, at] = total[q] + low_rows(low_in[1, q])

    for copy in copies:
        copy.wait_send()
    for role, leads in enumerate((lead, lead_mate)):

        @pl.when(leads)
        def _():
            for q in range(2):
                for copy in low_copies(role, q):
                    copy.wait_send()


def shards(valence, conduction, points, inverse_metric):
    rows, width = valence.shape
    count = points.shape[0]
    piece = count // 2 // NY
    lines = NX * NZL * NY
    out = pl.pallas_call(
        kernel,
        out_shape=jax.ShapeDtypeStruct((2, 2, NY, width), F32),
        in_specs=[pl.BlockSpec(memory_space=pltpu.HBM)] * 4,
        out_specs=pl.BlockSpec(memory_space=pltpu.VMEM),
        scratch_shapes=[
            pltpu.VMEM((1, count), jnp.int32),
            pltpu.VMEM((rows, width), BF16),
            pltpu.VMEM((rows, width), BF16),
            pltpu.VMEM((count, width), BF16),
            pltpu.VMEM((rows, width), BF16),
            pltpu.VMEM((rows, width), BF16),
            pltpu.VMEM((count, width), BF16),
            pltpu.VMEM((NY, 1, 2 * width), F32),
            pltpu.VMEM((NZL, NY, 2 * width), F32),
            pltpu.VMEM((NX, 2, NZL * NY // 2, 2 * width), BF16),
            pltpu.VMEM((2, NY, piece // 2, 2 * width), BF16),
            pltpu.VMEM((2, NY - 1, piece // 2, 2 * width), BF16),
            pltpu.VMEM((2, piece // 2, 2 * width), BF16),
            pltpu.VMEM((2, 3, piece // 2, 2 * width), BF16),
            pltpu.VMEM((2, 2, NY, 2, piece // 2, lines), BF16),
            pltpu.VMEM((lines, width), F32),
            pltpu.VMEM((2, NX, NZL * NY, width), BF16),
            pltpu.VMEM((2, NX - 1, NZL * NY, width), BF16),
            pltpu.VMEM((2, NZL, NX * NY, width), BF16),
            pltpu.VMEM((2, NZL - 1, NX * NY, width), BF16),
            pltpu.VMEM((2, NX, NZL, 2 * NY, width // 2), BF16),
            pltpu.VMEM((2, 2, 2 * NY, width // 2), BF16),
            pltpu.VMEM((2, NX, NY, width), F32),
            pltpu.VMEM((NX - 1, 2, NY, width), F32),
            pltpu.VMEM((2, NZL, NY, width), F32),
            pltpu.VMEM((NZL, 2, NY, width), F32),
            pltpu.SemaphoreType.DMA((COPIES,)),
            pltpu.SemaphoreType.DMA((COPIES,)),
            pltpu.SemaphoreType.DMA((4,)),
            pltpu.SemaphoreType.DMA((2, NX * NZL)),
            pltpu.SemaphoreType.DMA((2, 2)),
        ],
        compiler_params=pltpu.CompilerParams(
            collective_id=0, has_side_effects=True, vmem_limit_bytes=63 * 2**20
        ),
    )(points[None, :], valence, conduction, inverse_metric)
    return out.transpose(2, 1, 0, 3).reshape(NY * 4, width).astype(BF16)


def solution(mesh):
    return jax.shard_map(
        shards,
        mesh=mesh,
        in_specs=(
            P(("grid", "interp"), None),
            P(("grid", "interp"), None),
            P("grid"),
            P("grid", "interp"),
        ),
        out_specs=P("grid", "interp"),
        check_vma=False,
    )
```
